32 devices in a mesh: elec: 4 (over x, core), space: 8 (over z, y).
Axes of the slice: x: 2, y: 2, z: 4, core: 2. Of those that a mesh axis runs over, the one named last changes fastest.
Arguments:
- potentials: bfloat16 [2048, 16, 8, 128], P('elec', 'space'), may hold values from -6 to 6
- quadrupoles: int32 [4, 32768], replicated, may hold values from 0 to 2047
- residuals: float32 [32768], replicated, may hold values from -0.03125 to 0.03125
- cell_weight: float32 [16, 8, 128], P('space'), may hold values from 0.5 to 2
Outputs:
- model_gradient: float32 [16, 8, 128], P('space')
The draws below stay inside these ranges and needn't reach their ends.
All inputs are finite; a program needn't handle non-finite values.
Results may differ from the reference program's by a relative error of at most 0.0054.
Values may be sent and summed in bfloat16 or wider, within the bound.
No kernel may reach another device: no remote copies, remote signals or barrier semaphores. Data moves between devices by JAX's collectives and lax.ppermute only.
A program may use at most 192 MiB of HBM per device.

```python
import math
import jax
import jax.numpy as jnp
from jax import lax

E = 2048
NZ = 8
NY = 128
QUADS = 32768
NX = 16


def plant(entries, stream_key, smallest, top_value):
    place = [jax.random.randint(jax.random.fold_in(stream_key, axis), (), 0, length) for axis, length in enumerate(entries.shape)]
    main_axis = entries.shape.index(max(entries.shape))
    neighbour = place[:main_axis] + [(place[main_axis] + 1) % entries.shape[main_axis]] + place[main_axis + 1:]
    return entries.at[tuple(place)].set(smallest).at[tuple(neighbour)].set(top_value)


def steps_of(stream_key, dims, split, low, high):
    gain, own = 1.0, jax.random.fold_in(stream_key, 6)
    for dim, shards_of in split:
        steps = jnp.exp(jax.random.uniform(jax.random.fold_in(own, dim), (shards_of,), jnp.float32, low / len(split), high / len(split)))
        gain = gain * jnp.repeat(steps, dims[dim] // shards_of).reshape([-1 if axis == dim else 1 for axis in range(len(dims))])
    return gain


def normal_values(stream_key, shape, scale, reach, split=(), kind=jnp.bfloat16):
    factor_of = steps_of(stream_key, shape, split, -0.22, 0.18) if split else 1.0
    array = jax.random.normal(stream_key, shape, jnp.float32) * scale * factor_of
    return jnp.minimum(jnp.maximum(array, -reach), reach).astype(kind)


def setup_inputs(seed: int = 0) -> dict:
    key_of = jax.random.split(jax.random.key(seed), 5)
    potentials = normal_values(key_of[0], (E, NX, NZ, NY), 1.0, 6.0, ((0, 4), (1, 8)))
    quadrupoles = plant(jax.random.randint(key_of[1], (4, QUADS), 0, E), jax.random.fold_in(key_of[1], 1), 0, E - 1).astype(jnp.int32)
    residuals = normal_values(key_of[2], (QUADS,), QUADS ** -0.5, 0.03125, (), jnp.float32)
    cell_weight = jnp.clip(jnp.exp(math.log(2.0) - 1.3862944 * jax.random.uniform(key_of[3], (NX, NZ, NY), jnp.float32) ** steps_of(key_of[3], (NX, NZ, NY), ((0, 8),), -0.2, 0.2)), 0.5, 2.0)
    return {"potentials": potentials, "quadrupoles": quadrupoles, "residuals": residuals, "cell_weight": cell_weight}


def slopes_of(padded):
    field = padded.astype(jnp.float32)
    grad_x = 0.5 * (field[:, 2:] - field[:, :-2])
    inner = field[:, 1:-1]
    pad_z = jnp.pad(inner, ((0, 0), (0, 0), (1, 1), (0, 0)))
    grad_z = 0.5 * (pad_z[:, :, 2:] - pad_z[:, :, :-2])
    pad_y = jnp.pad(inner, ((0, 0), (0, 0), (0, 0), (1, 1)))
    grad_y = 0.5 * (pad_y[:, :, :, 2:] - pad_y[:, :, :, :-2])
    return jnp.stack([grad_x, grad_z, grad_y], axis=0).astype(jnp.bfloat16)


def coupling_rows(quadrupoles, residuals, first, count, width):
    source_a = quadrupoles[0]
    source_b = quadrupoles[1]
    probe_m = quadrupoles[2]
    probe_n = quadrupoles[3]
    rows = jnp.concatenate([source_a, source_a, source_b, source_b]) - first
    cols = jnp.concatenate([probe_m, probe_n, probe_m, probe_n])
    values = jnp.concatenate([residuals, -residuals, -residuals, residuals]).astype(jnp.float32)
    valid = (rows >= 0) & (rows < count)
    flat = jnp.where(valid, rows * width + cols, count * width).astype(jnp.int32)
    summed = jax.ops.segment_sum(values, flat, num_segments=count * width)
    return summed.reshape(count, width).astype(jnp.bfloat16)


def reference(potentials, quadrupoles, residuals, cell_weight):
    coupling = coupling_rows(quadrupoles, residuals, 0, E, E).astype(jnp.float32)
    padded = jnp.pad(potentials, ((0, 0), (1, 1), (0, 0), (0, 0)))

    def one_plane(index):
        window = lax.dynamic_slice_in_dim(padded, index, 3, 1)
        slopes = slopes_of(window).astype(jnp.float32)
        image = jnp.einsum("ef,kfxzy->kexzy", coupling, slopes, precision=lax.Precision.HIGHEST)
        return jnp.sum(slopes * image, axis=(0, 1))[0]

    planes = lax.map(one_plane, jnp.arange(NX, dtype=jnp.int32))
    return planes * cell_weight
```

```python
import jax
import jax.numpy as jnp
from jax import lax
from jax.experimental import pallas as pl
from jax.experimental.pallas import tpu as pltpu
from jax.sharding import Mesh, PartitionSpec as P

BLOCK = 256
CHUNK = 1024


def onehots(dest, base, rows, plus, minus, up, down):
    zero = jnp.zeros((16, CHUNK), jnp.bfloat16)
    for group in range(rows // 16):
        here = lax.broadcasted_iota(jnp.int16, (16, CHUNK), 0) + jnp.int16(16 * group)
        dest[pl.ds(16 * group, 16), pl.ds(base, CHUNK)] = jnp.where(
            plus == here, up, jnp.where(minus == here, down, zero)
        )


def segment(kind, index, cols, electrodes):
    if kind == "folded":
        return BLOCK + index * cols
    at = index * cols
    return jnp.where(at < BLOCK, at, at - BLOCK + electrodes // 2)


def coupling_kernel(kind, shape, place, quads, res, out, *hot):
    electrodes, rows, pairs, share = shape
    cols = out.shape[0]
    group = (2 * place[0] + place[3]) * pairs + place[2]
    row_base = (place[1] * rows + group // share) * BLOCK
    col_base = row_base + segment(kind, group % share, cols, electrodes)
    steps = quads.shape[1] // CHUNK

    def build(step, rows_hot, cols_hot):
        at = pl.ds(pl.multiple_of(step * CHUNK, CHUNK), CHUNK)
        number = [quads[i : i + 1, at] for i in range(4)]
        empty = (number[0] == number[1]) | (number[2] == number[3])
        value = jnp.where(empty, 0.0, res[0:1, at])
        value = jnp.broadcast_to(value, (16, CHUNK)).astype(jnp.bfloat16)
        one = jnp.ones((16, CHUNK), jnp.bfloat16)

        def wide(row, base):
            local = (row - base) & (electrodes - 1)
            return jnp.broadcast_to(local, (16, CHUNK)).astype(jnp.int16)

        ends = [(0, 1, 2, 3), (2, 3, 0, 1)][: 2 if kind == "folded" else 1]
        for index, (a, b, m, n) in enumerate(ends):
            onehots(rows_hot, index * CHUNK, BLOCK, wide(number[a], row_base), wide(number[b], row_base), one, -one)
            onehots(cols_hot, index * CHUNK, cols, wide(number[m], col_base), wide(number[n], col_base), value, -value)

    def multiply(rows_hot, cols_hot):
        return lax.dot_general(
            cols_hot[...],
            rows_hot[...],
            (((1,), (1,)), ((), ())),
            preferred_element_type=jnp.float32,
        )

    build(0, hot[0], hot[1])

    def pair(index, total):
        build(2 * index + 1, hot[2], hot[3])
        total = total + multiply(hot[0], hot[1])
        build(jnp.minimum(2 * index + 2, steps - 1), hot[0], hot[1])
        return total + multiply(hot[2], hot[3])

    total = lax.fori_loop(0, steps // 2, pair, jnp.zeros((cols, BLOCK), jnp.float32))
    out[...] = total.astype(jnp.bfloat16)


SMEM = pl.BlockSpec(memory_space=pltpu.SMEM)
VMEM = pl.BlockSpec(memory_space=pltpu.VMEM)


def coupling_piece(kind, place, quadrupoles, residuals, shape, cols):
    depth = (2 if kind == "folded" else 1) * CHUNK
    hot = [pltpu.VMEM((rows, depth), jnp.bfloat16) for rows in (BLOCK, cols, BLOCK, cols)]
    return pl.pallas_call(
        lambda *refs: coupling_kernel(kind, shape, *refs),
        out_shape=jax.ShapeDtypeStruct((cols, BLOCK), jnp.bfloat16),
        in_specs=[SMEM, VMEM, VMEM],
        out_specs=VMEM,
        scratch_shapes=hot,
        compiler_params=pltpu.CompilerParams(vmem_limit_bytes=16 << 20),
        cost_estimate=pl.CostEstimate(
            flops=2 * cols * BLOCK * quadrupoles.shape[1] * depth // CHUNK,
            bytes_accessed=1 << 20,
            transcendentals=0,
        ),
        name="coupling_" + kind,
    )(place, quadrupoles, residuals)


def assemble_kernel(rows, far, place, *refs):
    pieces, field = refs[:-1], refs[-1]
    electrodes = field.shape[1]
    tiles, count, _ = pieces[0].shape
    members = len(pieces) // len(far)
    for index, piece in enumerate(pieces):
        slot, k = index // members, index % members
        row = 1 - place[0] if far[slot] else place[0]
        member = (place[1] + members - k) % members
        first = (row * members + member) * count - place[1] * rows * BLOCK
        first = pl.multiple_of((first + electrodes) % electrodes, count)
        for tile in range(tiles):
            field[tiles * (slot // 2) + tile, pl.ds(first, count)] = piece[tile]


def assemble(place, pieces, far, rows, electrodes):
    tiles = pieces[0].shape[0]
    return pl.pallas_call(
        lambda *refs: assemble_kernel(rows, far, *refs),
        out_shape=jax.ShapeDtypeStruct((tiles * (len(far) // 2), electrodes, 128), jnp.bfloat16),
        in_specs=[SMEM] + [VMEM] * len(pieces),
        out_specs=VMEM,
        compiler_params=pltpu.CompilerParams(vmem_limit_bytes=16 << 20),
        cost_estimate=pl.CostEstimate(flops=0, bytes_accessed=4 << 20, transcendentals=0),
        name="assemble_fields",
    )(place, *pieces)


def gradient_kernel(shape, parts, last, place, field, before, *refs):
    electrodes, rows, pairs, share = shape
    arrays = refs[: len(parts)]
    out, joined, turned, image = refs[len(parts) :]
    tiles = field.shape[0] // 3
    window = turned.shape[1]
    for kind in ("folded", "shared"):
        for array, (far_row, far_par, lane, contents) in zip(arrays, parts):
            row = 1 - place[0] if far_row else place[0]
            par = 1 - place[3] if far_par else place[3]
            source = 0
            for held, cols in contents:
                for k in range(pairs):
                    group = (2 * row + par) * pairs + (place[2] + pairs - k) % pairs
                    if held == kind:
                        at = pl.multiple_of(segment(kind, group % share, cols, electrodes), 16)
                        joined[pl.ds(at, cols), pl.ds(lane, array.shape[2])] = array[k, source : source + cols]
                source += cols
    first = pl.multiple_of((group // share) * BLOCK, BLOCK)
    turned[...] = joined[:window].T
    for tile in range(0, 3 * tiles, 2):
        two = [field[tile + i, pl.ds(first, window)] for i in range(2)]
        both = jnp.dot(turned[...], jnp.concatenate(two, axis=1), preferred_element_type=jnp.float32)
        image[tile] = both[:, :128]
        image[tile + 1] = both[:, 128:]
    lane = lax.broadcasted_iota(jnp.int32, (16, 128), 1)

    def fold(product):
        return product[:8] + product[8:]

    def along(value):
        return jnp.where(lane == 0, 0.0, value) - jnp.where(lane == 1, 0.0, pltpu.roll(value, 2, 1))

    nothing = jnp.zeros((1, 128), jnp.float32)
    for plane in range(2):

        def step(index, totals):
            at = pl.multiple_of(index * 16, 16)
            u = [
                field[tiles * plane + j, pl.ds(first + at, 16)].astype(jnp.float32)
                for j in range(2 * tiles)
            ]
            v = [image[tiles * plane + j, pl.ds(at, 16)] for j in range(2 * tiles)]
            new = []
            for j in range(tiles):
                new.append(fold(along(u[j]) * along(v[j])))
            for j in range(tiles - 1):
                new.append(fold((u[j] - u[j + 1]) * (v[j] - v[j + 1])))
            new.append(fold(u[tiles - 1] * v[tiles - 1]))
            for j in range(tiles):
                new.append(fold((u[j] - u[j + tiles]) * (v[j] - v[j + tiles])))
            return tuple(a + b for a, b in zip(totals, new))

        base = 3 * tiles * plane
        totals = lax.fori_loop(0, BLOCK // 16, step, tuple(before[base + j] for j in range(3 * tiles)))
        if not last:
            for j in range(3 * tiles):
                out[base + j] = totals[j]
            continue
        total = [0.25 * jnp.sum(value, axis=0, keepdims=True) for value in totals]
        for j in range(tiles):
            out[2 * plane, 2 * j : 2 * j + 1] = pltpu.roll(total[j], 127, 1)
            out[2 * plane, 2 * j + 1 : 2 * j + 2] = total[tiles + j]
            out[2 * plane + 1, 2 * j : 2 * j + 1] = total[2 * tiles + j]
            out[2 * plane + 1, 2 * j + 1 : 2 * j + 2] = nothing


def gradient_sums(place, field, before, entries, shape, window, last):
    arrays = [entry[0] for entry in entries]
    parts = [entry[1:] for entry in entries]
    tiles = field.shape[0] // 3
    folded = max(cols for part in parts for kind, cols in part[3] if kind == "folded")
    covered = max(window, BLOCK + shape[3] * folded)
    size = (4, 2 * tiles, 128) if last else before.shape
    return pl.pallas_call(
        lambda *refs: gradient_kernel(shape, parts, last, *refs),
        out_shape=jax.ShapeDtypeStruct(size, jnp.float32),
        in_specs=[SMEM, VMEM, VMEM] + [VMEM] * len(arrays),
        out_specs=VMEM,
        scratch_shapes=[
            pltpu.VMEM((covered, BLOCK), jnp.bfloat16),
            pltpu.VMEM((BLOCK, window), jnp.bfloat16),
            pltpu.VMEM((3 * tiles, BLOCK, 128), jnp.float32),
        ],
        compiler_params=pltpu.CompilerParams(vmem_limit_bytes=16 << 20),
        cost_estimate=pl.CostEstimate(
            flops=2 * BLOCK * window * 3 * tiles * 128, bytes_accessed=8 << 20, transcendentals=0
        ),
        name="gradient_sums",
    )(place, field, before, *arrays)


def rotations(value, axis):
    size = lax.axis_size(axis)
    return [
        lax.ppermute(value, axis, [(i, (i + k) % size) for i in range(size)]) for k in range(1, size)
    ]


def local(potentials, quadrupoles, residuals, cell_weight):
    count = potentials.shape[0]
    row, mem = lax.axis_index("row"), lax.axis_index("mem")
    pair, par = lax.axis_index("pair"), lax.axis_index("par")
    members, pairs = lax.axis_size("mem"), lax.axis_size("pair")
    electrodes = 2 * members * count
    rows = electrodes // BLOCK // members
    window = electrodes // 2 + BLOCK
    share = 4 * pairs // rows
    folded = -(-(window - 2 * BLOCK) // (16 * share)) * 16
    shared = 2 * BLOCK // share
    shape = (electrodes, rows, pairs, share)
    place = jnp.stack([row, mem, pair, par]).astype(jnp.int32)

    planes = jnp.transpose(potentials, (1, 2, 0, 3))
    even, odd = planes[:, 0::2], planes[:, ::-1][:, 0::2]
    mine = jnp.where(row == 0, even, odd)
    theirs = jnp.where(row == 0, odd, even)
    native, native_out = (jnp.where(par == 0, a[0], a[1]) for a in (mine, theirs))
    other, other_out = (jnp.where(par == 0, a[1], a[0]) for a in (mine, theirs))
    swap = [(0, 1), (1, 0)]
    ring = [(i, i - 1, 0) for i in range(1, pairs)] + [(i, i + 1, 1) for i in range(pairs - 1)]
    ahead = [(2 * a + p, 2 * b + p) for a, b, p in ring]
    ahead_across = [
        (2 * pairs * r + a, 2 * pairs * (1 - r) + b) for r in range(2) for a, b in ahead
    ]
    relay = lax.ppermute(other_out, "par", swap)
    first = [
        lax.ppermute(native_out, "row", swap),
        lax.ppermute(other, "par", swap),
        lax.ppermute(native_out, ("row", "pair", "par"), ahead_across),
        lax.ppermute(native, ("pair", "par"), ahead),
    ]
    inputs = (place, quadrupoles, residuals.reshape(1, -1), shape)

    piece = coupling_piece("folded", *inputs, folded)
    relay, first, _ = lax.optimization_barrier((relay, first, piece))
    second_across = lax.ppermute(relay, "row", swap)
    turns = rotations(piece, "pair")
    shared_piece = coupling_piece("shared", *inputs, shared)
    shared_turns = rotations(shared_piece, "pair")
    moved = second_across, first, native, turns
    (second_across, first, native, turns), _ = lax.optimization_barrier((moved, shared_piece))
    column = jnp.stack([piece] + turns)
    by_row = lax.ppermute(column, "row", swap)
    by_par = lax.ppermute(column, "par", swap)

    moved = second_across, first, native, shared_turns, by_row, by_par
    second_across, first, native, shared_turns, by_row, by_par = lax.optimization_barrier(moved)
    across, second, halo_across, halo = first
    tiles = native.shape[0]
    pieces = []
    for array in (native, across, second, second_across, halo, halo_across):
        pieces += [array] + rotations(array, "mem")
    field = assemble(place, pieces, (0, 1, 0, 1, 0, 1), rows, electrodes)
    shared_column = jnp.stack([shared_piece] + shared_turns)
    shared_by_row = lax.ppermute(shared_column, "row", swap)
    shared_by_par = lax.ppermute(shared_column, "par", swap)

    def entries(part, shared_part, far_row, far_par):
        return [
            (part, far_row, far_par, 0, (("folded", folded),)),
            (shared_part, far_row, far_par, 0, (("shared", shared),)),
        ]

    sums = jnp.zeros((6 * tiles, 8, 128), jnp.float32)
    near = entries(column, shared_column, 0, 0)
    staged = rows == 4
    arrived = by_row, by_par, shared_by_row, shared_by_par
    if staged:
        sums = gradient_sums(place, field, sums, near, shape, window, False)
        arrived, sums = lax.optimization_barrier((arrived, sums))
    by_row, by_par, shared_by_row, shared_by_par = arrived
    beside = entries(by_row, shared_by_row, 1, 0), entries(by_par, shared_by_par, 0, 1)
    half = BLOCK // 2
    lower = jnp.concatenate([by_row[..., :half], shared_by_row[..., :half]], axis=1)
    upper = jnp.concatenate([by_par[..., half:], shared_by_par[..., half:]], axis=1)
    corner = lax.ppermute(lower, "par", swap), lax.ppermute(upper, "row", swap)
    if staged:
        for part in beside:
            sums = gradient_sums(place, field, sums, part, shape, window, False)
        corner, sums = lax.optimization_barrier((corner, sums))
    contents = (("folded", folded), ("shared", shared))
    far = [(corner[0], 1, 1, 0, contents), (corner[1], 1, 1, half, contents)]
    part = far if staged else near + beside[0] + beside[1] + far
    sums = gradient_sums(place, field, sums, part, shape, window, True)

    sums = jnp.where(par == 0, sums, sums[::-1])
    sums = jnp.where(row == 0, sums, sums[:, ::-1])
    total = jnp.where(par == 0, sums[:2], sums[2:])
    total = total + lax.ppermute(jnp.where(par == 0, sums[2:], sums[:2]), "par", swap)
    total = total + lax.ppermute(total, "row", swap)
    for turn in rotations(total, "mem"):
        total = total + turn
    return total * cell_weight


def solution(mesh):
    elec, space = mesh.devices.shape
    names = ("row", "mem", "pair", "par")
    finer = Mesh(mesh.devices.reshape(2, elec // 2, space // 2, 2), names)
    e, s = names[:2], names[2:]
    placed = (P(e, s, None, None), P(), P(), P(s, None, None))
    return jax.shard_map(local, mesh=finer, in_specs=placed, out_specs=P(s, None, None), check_vma=False)
```

```python
import jax
import jax.numpy as jnp
from jax import lax
from jax.experimental import pallas as pl
from jax.experimental.pallas import tpu as pltpu
from jax.sharding import Mesh, PartitionSpec as P

BLOCK = 256
CHUNK = 1024


def onehots(dest, first, rows, plus, minus, up, down):
    zero = jnp.zeros((16, CHUNK), jnp.bfloat16)
    for group in range(rows // 16):
        here = lax.broadcasted_iota(jnp.int16, (16, CHUNK), 0) + jnp.int16(16 * group)
        dest[pl.ds(first + 16 * group, 16)] = jnp.where(
            plus == here, up, jnp.where(minus == here, down, zero)
        )


def segment(kind, index, cols, electrodes):
    if kind == "folded":
        return BLOCK + index * cols
    at = index * cols
    return jnp.where(at < BLOCK, at, at - BLOCK + electrodes // 2)


def coupling_kernel(shape, place, quads, res, out, *hot):
    electrodes, rows, pairs, share, folded, shared = shape
    group = (2 * place[0] + place[3]) * pairs + place[2]
    row_base = (place[1] * rows + group // share) * BLOCK
    folded_base = row_base + segment("folded", group % share, folded, electrodes)
    shared_base = row_base + segment("shared", group % share, shared, electrodes)
    steps = quads.shape[1] // CHUNK

    def build(step, near_hot, far_hot, cols_hot, back_hot):
        at = pl.ds(pl.multiple_of(step * CHUNK, CHUNK), CHUNK)
        number = [quads[i : i + 1, at] for i in range(4)]
        empty = (number[0] == number[1]) | (number[2] == number[3])
        value = jnp.where(empty, 0.0, res[0:1, at])
        value = jnp.broadcast_to(value, (16, CHUNK)).astype(jnp.bfloat16)
        one = jnp.ones((16, CHUNK), jnp.bfloat16)

        def wide(row, base):
            local = (row - base) & (electrodes - 1)
            return jnp.broadcast_to(local, (16, CHUNK)).astype(jnp.int16)

        a, b, m, n = number
        onehots(near_hot, 0, BLOCK, wide(a, row_base), wide(b, row_base), one, -one)
        onehots(far_hot, 0, BLOCK, wide(m, row_base), wide(n, row_base), one, -one)
        onehots(cols_hot, 0, folded, wide(m, folded_base), wide(n, folded_base), value, -value)
        onehots(cols_hot, folded, shared, wide(m, shared_base), wide(n, shared_base), value, -value)
        onehots(back_hot, 0, folded, wide(a, folded_base), wide(b, folded_base), value, -value)

    def multiply(near_hot, far_hot, cols_hot, back_hot):
        dims = (((1,), (1,)), ((), ()))
        ahead = lax.dot_general(cols_hot[...], near_hot[...], dims, preferred_element_type=jnp.float32)
        back = lax.dot_general(back_hot[...], far_hot[...], dims, preferred_element_type=jnp.float32)
        return ahead[:folded] + back, ahead[folded:]

    def add(total, new):
        return total[0] + new[0], total[1] + new[1]

    build(0, *hot[:4])

    def pair(index, total):
        build(2 * index + 1, *hot[4:])
        total = add(total, multiply(*hot[:4]))
        build(jnp.minimum(2 * index + 2, steps - 1), *hot[:4])
        return add(total, multiply(*hot[4:]))

    zeros = jnp.zeros((folded, BLOCK), jnp.float32), jnp.zeros((shared, BLOCK), jnp.float32)
    total = lax.fori_loop(0, steps // 2, pair, zeros)
    out[:folded] = total[0].astype(jnp.bfloat16)
    out[folded:] = total[1].astype(jnp.bfloat16)


SMEM = pl.BlockSpec(memory_space=pltpu.SMEM)
VMEM = pl.BlockSpec(memory_space=pltpu.VMEM)


def coupling_piece(place, quadrupoles, residuals, shape):
    folded, shared = shape[4:]
    hot = [pltpu.VMEM((rows, CHUNK), jnp.bfloat16) for rows in (BLOCK, BLOCK, folded + shared, folded)]
    return pl.pallas_call(
        lambda *refs: coupling_kernel(shape, *refs),
        out_shape=jax.ShapeDtypeStruct((folded + shared, BLOCK), jnp.bfloat16),
        in_specs=[SMEM, VMEM, VMEM],
        out_specs=VMEM,
        scratch_shapes=hot + hot,
        compiler_params=pltpu.CompilerParams(vmem_limit_bytes=16 << 20),
        cost_estimate=pl.CostEstimate(
            flops=2 * (2 * folded + shared) * BLOCK * quadrupoles.shape[1],
            bytes_accessed=1 << 20,
            transcendentals=0,
        ),
        name="coupling_piece",
    )(place, quadrupoles, residuals)


def assemble_kernel(rows, far, place, *refs):
    pieces, field = refs[:-1], refs[-1]
    electrodes = field.shape[1]
    tiles, count, _ = pieces[0].shape
    members = len(pieces) // len(far)
    for index, piece in enumerate(pieces):
        slot, k = index // members, index % members
        row = 1 - place[0] if far[slot] else place[0]
        member = (place[1] + members - k) % members
        first = (row * members + member) * count - place[1] * rows * BLOCK
        first = pl.multiple_of((first + electrodes) % electrodes, count)
        for tile in range(tiles):
            field[tiles * (slot // 2) + tile, pl.ds(first, count)] = piece[tile]


def assemble(place, pieces, far, rows, electrodes):
    tiles = pieces[0].shape[0]
    return pl.pallas_call(
        lambda *refs: assemble_kernel(rows, far, *refs),
        out_shape=jax.ShapeDtypeStruct((tiles * (len(far) // 2), electrodes, 128), jnp.bfloat16),
        in_specs=[SMEM] + [VMEM] * len(pieces),
        out_specs=VMEM,
        compiler_params=pltpu.CompilerParams(vmem_limit_bytes=16 << 20),
        cost_estimate=pl.CostEstimate(flops=0, bytes_accessed=4 << 20, transcendentals=0),
        name="assemble_fields",
    )(place, *pieces)


def gradient_kernel(shape, parts, last, place, field, before, *refs):
    electrodes, rows, pairs, share, folded, shared = shape
    arrays = refs[: len(parts)]
    out, joined, turned, image = refs[len(parts) :]
    tiles = field.shape[0] // 3
    window = turned.shape[1]
    for kind, source, cols in (("folded", 0, folded), ("shared", folded, shared)):
        for array, (far_row, far_par, lane) in zip(arrays, parts):
            row = 1 - place[0] if far_row else place[0]
            par = 1 - place[3] if far_par else place[3]
            for k in range(pairs):
                group = (2 * row + par) * pairs + (place[2] + pairs - k) % pairs
                at = pl.multiple_of(segment(kind, group % share, cols, electrodes), 16)
                joined[pl.ds(at, cols), pl.ds(lane, array.shape[2])] = array[k, source : source + cols]
    first = pl.multiple_of((group // share) * BLOCK, BLOCK)
    turned[...] = joined[:window].T
    for tile in range(0, 3 * tiles, 2):
        two = [field[tile + i, pl.ds(first, window)] for i in range(2)]
        both = jnp.dot(turned[...], jnp.concatenate(two, axis=1), preferred_element_type=jnp.float32)
        image[tile] = both[:, :128]
        image[tile + 1] = both[:, 128:]
    lane = lax.broadcasted_iota(jnp.int32, (16, 128), 1)

    def fold(product):
        return product[:8] + product[8:]

    def along(value):
        return jnp.where(lane == 0, 0.0, value) - jnp.where(lane == 1, 0.0, pltpu.roll(value, 2, 1))

    nothing = jnp.zeros((1, 128), jnp.float32)
    for plane in range(2):

        def step(index, totals):
            at = pl.multiple_of(index * 16, 16)
            u = [
                field[tiles * plane + j, pl.ds(first + at, 16)].astype(jnp.float32)
                for j in range(2 * tiles)
            ]
            v = [image[tiles * plane + j, pl.ds(at, 16)] for j in range(2 * tiles)]
            new = []
            for j in range(tiles):
                new.append(fold(along(u[j]) * along(v[j])))
            for j in range(tiles - 1):
                new.append(fold((u[j] - u[j + 1]) * (v[j] - v[j + 1])))
            new.append(fold(u[tiles - 1] * v[tiles - 1]))
            for j in range(tiles):
                new.append(fold((u[j] - u[j + tiles]) * (v[j] - v[j + tiles])))
            return tuple(a + b for a, b in zip(totals, new))

        base = 3 * tiles * plane
        start = tuple(before[base + j] for j in range(3 * tiles))
        totals = lax.fori_loop(0, BLOCK // 16, step, start, unroll=4)
        if not last:
            for j in range(3 * tiles):
                out[base + j] = totals[j]
            continue
        total = [0.25 * jnp.sum(value, axis=0, keepdims=True) for value in totals]
        for j in range(tiles):
            out[2 * plane, 2 * j : 2 * j + 1] = pltpu.roll(total[j], 127, 1)
            out[2 * plane, 2 * j + 1 : 2 * j + 2] = total[tiles + j]
            out[2 * plane + 1, 2 * j : 2 * j + 1] = total[2 * tiles + j]
            out[2 * plane + 1, 2 * j + 1 : 2 * j + 2] = nothing


def gradient_sums(place, field, before, entries, shape, window, last):
    arrays = [entry[0] for entry in entries]
    parts = [entry[1:] for entry in entries]
    tiles = field.shape[0] // 3
    covered = max(window, BLOCK + shape[3] * shape[4])
    size = (4, 2 * tiles, 128) if last else before.shape
    return pl.pallas_call(
        lambda *refs: gradient_kernel(shape, parts, last, *refs),
        out_shape=jax.ShapeDtypeStruct(size, jnp.float32),
        in_specs=[SMEM, VMEM, VMEM] + [VMEM] * len(arrays),
        out_specs=VMEM,
        scratch_shapes=[
            pltpu.VMEM((covered, BLOCK), jnp.bfloat16),
            pltpu.VMEM((BLOCK, window), jnp.bfloat16),
            pltpu.VMEM((3 * tiles, BLOCK, 128), jnp.float32),
        ],
        compiler_params=pltpu.CompilerParams(vmem_limit_bytes=16 << 20),
        cost_estimate=pl.CostEstimate(
            flops=2 * BLOCK * window * 3 * tiles * 128, bytes_accessed=8 << 20, transcendentals=0
        ),
        name="gradient_sums",
    )(place, field, before, *arrays)


def rotations(value, axis):
    size = lax.axis_size(axis)
    return [
        lax.ppermute(value, axis, [(i, (i + k) % size) for i in range(size)]) for k in range(1, size)
    ]


def local(potentials, quadrupoles, residuals, cell_weight):
    count = potentials.shape[0]
    row, mem = lax.axis_index("row"), lax.axis_index("mem")
    pair, par = lax.axis_index("pair"), lax.axis_index("par")
    members, pairs = lax.axis_size("mem"), lax.axis_size("pair")
    electrodes = 2 * members * count
    rows = electrodes // BLOCK // members
    window = electrodes // 2 + BLOCK
    share = 4 * pairs // rows
    folded = -(-(window - 2 * BLOCK) // (16 * share)) * 16
    shared = 2 * BLOCK // share
    shape = (electrodes, rows, pairs, share, folded, shared)
    place = jnp.stack([row, mem, pair, par]).astype(jnp.int32)

    planes = jnp.transpose(potentials, (1, 2, 0, 3))
    even, odd = planes[:, 0::2], planes[:, ::-1][:, 0::2]
    mine = jnp.where(row == 0, even, odd)
    theirs = jnp.where(row == 0, odd, even)
    native, native_out = (jnp.where(par == 0, a[0], a[1]) for a in (mine, theirs))
    other, other_out = (jnp.where(par == 0, a[1], a[0]) for a in (mine, theirs))
    tiles = native.shape[0]
    swap = [(0, 1), (1, 0)]
    ahead = [(2 * i, 2 * i - 2) for i in range(1, pairs)] + [(2 * i + 1, 2 * i + 3) for i in range(pairs - 1)]
    ahead_across = [(2 * pairs * r + a, 2 * pairs * (1 - r) + b) for r in range(2) for a, b in ahead]
    first = [
        lax.ppermute(other_out, "par", swap),
        lax.ppermute(native_out, "row", swap),
        lax.ppermute(native_out, ("row", "pair", "par"), ahead_across),
        lax.ppermute(native, ("pair", "par"), ahead),
    ]
    piece = coupling_piece(place, quadrupoles, residuals.reshape(1, -1), shape)
    turns = rotations(piece, "pair")
    (relay, across, halo_across, halo), other, _ = lax.optimization_barrier((first, other, piece))
    second_across = lax.ppermute(relay, "row", swap)
    second = lax.ppermute(other, "par", swap)
    moved = native, across, second, second_across, halo, halo_across, turns
    *held, turns = lax.optimization_barrier(moved)

    column = jnp.stack([piece] + turns)
    by_row = lax.ppermute(column, "row", swap)
    by_par = lax.ppermute(column, "par", swap)
    pieces = []
    for array in held:
        pieces += [array] + rotations(array, "mem")
    field = assemble(place, pieces, (0, 1, 0, 1, 0, 1), rows, electrodes)

    sums = jnp.zeros((6 * tiles, 8, 128), jnp.float32)
    half = BLOCK // 2
    near = [(column, 0, 0, 0)]
    staged = rows == 4
    if staged:
        sums = gradient_sums(place, field, sums, near, shape, window, False)
        by_row, by_par, sums = lax.optimization_barrier((by_row, by_par, sums))
    corner = [
        lax.ppermute(by_row[..., :half], "par", swap),
        lax.ppermute(by_par[..., half:], "row", swap),
    ]
    beside = [[(by_row, 1, 0, 0)], [(by_par, 0, 1, 0)]]
    if staged:
        for part in beside:
            sums = gradient_sums(place, field, sums, part, shape, window, False)
        corner, sums = lax.optimization_barrier((corner, sums))
    far = [(corner[0], 1, 1, 0), (corner[1], 1, 1, half)]
    part = far if staged else near + beside[0] + beside[1] + far
    sums = gradient_sums(place, field, sums, part, shape, window, True)

    sums = jnp.where(par == 0, sums, sums[::-1])
    sums = jnp.where(row == 0, sums, sums[:, ::-1])
    kept = jnp.where(par == 0, sums[:2], sums[2:])
    given = jnp.where(par == 0, sums[2:], sums[:2])
    total = kept + lax.ppermute(kept, "row", swap) + lax.ppermute(given, "par", swap)
    total = total + lax.ppermute(given, ("row", "par"), [(0, 3), (1, 2), (2, 1), (3, 0)])
    for turn in rotations(total, "mem"):
        total = total + turn
    return total * cell_weight


def solution(mesh):
    elec, space = mesh.devices.shape
    names = ("row", "mem", "pair", "par")
    finer = Mesh(mesh.devices.reshape(2, elec // 2, space // 2, 2), names)
    e, s = names[:2], names[2:]
    placed = (P(e, s, None, None), P(), P(), P(s, None, None))
    return jax.shard_map(local, mesh=finer, in_specs=placed, out_specs=P(s, None, None), check_vma=False)
```

```python
import jax
import jax.numpy as jnp
from jax import lax
from jax.experimental import pallas as pl
from jax.experimental.pallas import tpu as pltpu
from jax.sharding import Mesh, PartitionSpec as P

BLOCK = 256
CHUNK = 512


def onehots(dest, first, rows, plus, minus, up, down):
    zero = jnp.zeros((16, CHUNK), jnp.bfloat16)
    for group in range(rows // 16):
        here = lax.broadcasted_iota(jnp.int16, (16, CHUNK), 0) + jnp.int16(16 * group)
        dest[pl.ds(first + 16 * group, 16)] = jnp.where(
            plus == here, up, jnp.where(minus == here, down, zero)
        )


def segment(kind, index, cols, electrodes):
    if kind == "folded":
        return BLOCK + index * cols
    at = index * cols
    return jnp.where(at < BLOCK, at, at - BLOCK + electrodes // 2)


def coupling_kernel(shape, place, quads, res, out, *hot):
    electrodes, rows, pairs, share, folded, shared = shape
    group = (2 * place[0] + place[3]) * pairs + place[2]
    row_base = (place[1] * rows + group // share) * BLOCK
    folded_base = row_base + segment("folded", group % share, folded, electrodes)
    shared_base = row_base + segment("shared", group % share, shared, electrodes)
    steps = quads.shape[1] // CHUNK

    def build(step, near_hot, far_hot, cols_hot, back_hot):
        at = pl.ds(pl.multiple_of(step * CHUNK, CHUNK), CHUNK)
        number = [quads[i : i + 1, at] for i in range(4)]
        empty = (number[0] == number[1]) | (number[2] == number[3])
        value = jnp.where(empty, 0.0, res[0:1, at])
        value = jnp.broadcast_to(value, (16, CHUNK)).astype(jnp.bfloat16)
        one = jnp.ones((16, CHUNK), jnp.bfloat16)

        def wide(row, base):
            local = (row - base) & (electrodes - 1)
            return jnp.broadcast_to(local, (16, CHUNK)).astype(jnp.int16)

        a, b, m, n = number
        onehots(near_hot, 0, BLOCK, wide(a, row_base), wide(b, row_base), one, -one)
        onehots(far_hot, 0, BLOCK, wide(m, row_base), wide(n, row_base), one, -one)
        onehots(cols_hot, 0, folded, wide(m, folded_base), wide(n, folded_base), value, -value)
        onehots(cols_hot, folded, shared, wide(m, shared_base), wide(n, shared_base), value, -value)
        onehots(back_hot, 0, folded, wide(a, folded_base), wide(b, folded_base), value, -value)

    def multiply(near_hot, far_hot, cols_hot, back_hot):
        dims = (((1,), (1,)), ((), ()))
        ahead = lax.dot_general(cols_hot[...], near_hot[...], dims, preferred_element_type=jnp.float32)
        back = lax.dot_general(back_hot[...], far_hot[...], dims, preferred_element_type=jnp.float32)
        return ahead[:folded] + back, ahead[folded:]

    def add(total, new):
        return total[0] + new[0], total[1] + new[1]

    build(0, *hot[:4])

    def pair(index, total):
        build(2 * index + 1, *hot[4:])
        total = add(total, multiply(*hot[:4]))
        build(jnp.minimum(2 * index + 2, steps - 1), *hot[:4])
        return add(total, multiply(*hot[4:]))

    zeros = jnp.zeros((folded, BLOCK), jnp.float32), jnp.zeros((shared, BLOCK), jnp.float32)
    total = lax.fori_loop(0, steps // 2, pair, zeros)
    out[:folded] = total[0].astype(jnp.bfloat16)
    out[folded:] = total[1].astype(jnp.bfloat16)


SMEM = pl.BlockSpec(memory_space=pltpu.SMEM)
VMEM = pl.BlockSpec(memory_space=pltpu.VMEM)


def coupling_piece(place, quadrupoles, residuals, shape):
    folded, shared = shape[4:]
    hot = [pltpu.VMEM((rows, CHUNK), jnp.bfloat16) for rows in (BLOCK, BLOCK, folded + shared, folded)]
    return pl.pallas_call(
        lambda *refs: coupling_kernel(shape, *refs),
        out_shape=jax.ShapeDtypeStruct((folded + shared, BLOCK), jnp.bfloat16),
        in_specs=[SMEM, VMEM, VMEM],
        out_specs=VMEM,
        scratch_shapes=hot + hot,
        compiler_params=pltpu.CompilerParams(vmem_limit_bytes=16 << 20),
        cost_estimate=pl.CostEstimate(
            flops=2 * (2 * folded + shared) * BLOCK * quadrupoles.shape[1],
            bytes_accessed=1 << 20,
            transcendentals=0,
        ),
        name="coupling_piece",
    )(place, quadrupoles, residuals)


def assemble_kernel(rows, far, place, *refs):
    pieces, field = refs[:-1], refs[-1]
    electrodes = field.shape[1]
    members = len(pieces)
    total, count, _ = pieces[0].shape
    tiles = total // len(far)
    for k, piece in enumerate(pieces):
        member = (place[1] + members - k) % members
        for slot, other in enumerate(far):
            row = 1 - place[0] if other else place[0]
            first = (row * members + member) * count - place[1] * rows * BLOCK
            first = pl.multiple_of((first + electrodes) % electrodes, count)
            for tile in range(tiles):
                field[tiles * (slot // 2) + tile, pl.ds(first, count)] = piece[tiles * slot + tile]


def assemble(place, pieces, far, rows, electrodes):
    return pl.pallas_call(
        lambda *refs: assemble_kernel(rows, far, *refs),
        out_shape=jax.ShapeDtypeStruct((pieces[0].shape[0] // 2, electrodes, 128), jnp.bfloat16),
        in_specs=[SMEM] + [VMEM] * len(pieces),
        out_specs=VMEM,
        compiler_params=pltpu.CompilerParams(vmem_limit_bytes=16 << 20),
        cost_estimate=pl.CostEstimate(flops=0, bytes_accessed=4 << 20, transcendentals=0),
        name="assemble_fields",
    )(place, *pieces)


def gradient_kernel(shape, parts, last, place, field, before, *refs):
    electrodes, rows, pairs, share, folded, shared = shape
    arrays = refs[: len(parts)]
    out, joined, turned, image = refs[len(parts) :]
    tiles = field.shape[0] // 3
    window = turned.shape[1]
    for kind, source, cols in (("folded", 0, folded), ("shared", folded, shared)):
        for array, (far_row, far_par, lane, turn) in zip(arrays, parts):
            row = 1 - place[0] if far_row else place[0]
            par = 1 - place[3] if far_par else place[3]
            for k in range(array.shape[0]):
                group = (2 * row + par) * pairs + (place[2] + pairs - turn - k) % pairs
                at = pl.multiple_of(segment(kind, group % share, cols, electrodes), 16)
                joined[pl.ds(at, cols), pl.ds(lane, array.shape[2])] = array[k, source : source + cols]
    first = pl.multiple_of((group // share) * BLOCK, BLOCK)
    turned[...] = joined[:window].T
    for tile in range(0, 3 * tiles, 2):
        two = [field[tile + i, pl.ds(first, window)] for i in range(2)]
        both = jnp.dot(turned[...], jnp.concatenate(two, axis=1), preferred_element_type=jnp.float32)
        image[tile] = both[:, :128]
        image[tile + 1] = both[:, 128:]
    lane = lax.broadcasted_iota(jnp.int32, (16, 128), 1)

    def fold(product):
        return product[:8] + product[8:]

    def along(value):
        return jnp.where(lane == 0, 0.0, value) - jnp.where(lane == 1, 0.0, pltpu.roll(value, 2, 1))

    nothing = jnp.zeros((1, 128), jnp.float32)
    for plane in range(2):

        def step(index, totals):
            at = pl.multiple_of(index * 16, 16)
            u = [
                field[tiles * plane + j, pl.ds(first + at, 16)].astype(jnp.float32)
                for j in range(2 * tiles)
            ]
            v = [image[tiles * plane + j, pl.ds(at, 16)] for j in range(2 * tiles)]
            new = []
            for j in range(tiles):
                new.append(fold(along(u[j]) * along(v[j])))
            for j in range(tiles - 1):
                new.append(fold((u[j] - u[j + 1]) * (v[j] - v[j + 1])))
            new.append(fold(u[tiles - 1] * v[tiles - 1]))
            for j in range(tiles):
                new.append(fold((u[j] - u[j + tiles]) * (v[j] - v[j + tiles])))
            return tuple(a + b for a, b in zip(totals, new))

        base = 3 * tiles * plane
        start = tuple(before[base + j] for j in range(3 * tiles))
        totals = lax.fori_loop(0, BLOCK // 16, step, start, unroll=8)
        if not last:
            for j in range(3 * tiles):
                out[base + j] = totals[j]
            continue
        total = [0.25 * jnp.sum(value, axis=0, keepdims=True) for value in totals]
        for j in range(tiles):
            out[2 * plane, 2 * j : 2 * j + 1] = pltpu.roll(total[j], 127, 1)
            out[2 * plane, 2 * j + 1 : 2 * j + 2] = total[tiles + j]
            out[2 * plane + 1, 2 * j : 2 * j + 1] = total[2 * tiles + j]
            out[2 * plane + 1, 2 * j + 1 : 2 * j + 2] = nothing


def gradient_sums(place, field, before, entries, shape, window, last):
    arrays = [entry[0] for entry in entries]
    parts = [entry[1:] for entry in entries]
    tiles = field.shape[0] // 3
    covered = max(window, BLOCK + shape[3] * shape[4])
    size = (4, 2 * tiles, 128) if last else before.shape
    return pl.pallas_call(
        lambda *refs: gradient_kernel(shape, parts, last, *refs),
        out_shape=jax.ShapeDtypeStruct(size, jnp.float32),
        in_specs=[SMEM, VMEM, VMEM] + [VMEM] * len(arrays),
        out_specs=VMEM,
        scratch_shapes=[
            pltpu.VMEM((covered, BLOCK), jnp.bfloat16),
            pltpu.VMEM((BLOCK, window), jnp.bfloat16),
            pltpu.VMEM((3 * tiles, BLOCK, 128), jnp.float32),
        ],
        compiler_params=pltpu.CompilerParams(vmem_limit_bytes=16 << 20),
        cost_estimate=pl.CostEstimate(
            flops=2 * BLOCK * window * 3 * tiles * 128, bytes_accessed=8 << 20, transcendentals=0
        ),
        name="gradient_sums",
    )(place, field, before, *arrays)


def rotations(value, axis):
    size = lax.axis_size(axis)
    return [
        lax.ppermute(value, axis, [(i, (i + k) % size) for i in range(size)]) for k in range(1, size)
    ]


def local(potentials, quadrupoles, residuals, cell_weight):
    count = potentials.shape[0]
    row, mem = lax.axis_index("row"), lax.axis_index("mem")
    pair, par = lax.axis_index("pair"), lax.axis_index("par")
    members, pairs = lax.axis_size("mem"), lax.axis_size("pair")
    electrodes = 2 * members * count
    rows = electrodes // BLOCK // members
    window = electrodes // 2 + BLOCK
    share = 4 * pairs // rows
    folded = -(-(window - 2 * BLOCK) // (16 * share)) * 16
    shared = 2 * BLOCK // share
    shape = (electrodes, rows, pairs, share, folded, shared)
    place = jnp.stack([row, mem, pair, par]).astype(jnp.int32)

    planes = jnp.transpose(potentials, (1, 2, 0, 3))
    even, odd = planes[:, 0::2], planes[:, ::-1][:, 0::2]
    mine = jnp.where(row == 0, even, odd)
    theirs = jnp.where(row == 0, odd, even)
    native, native_out = (jnp.where(par == 0, a[0], a[1]) for a in (mine, theirs))
    other, other_out = (jnp.where(par == 0, a[1], a[0]) for a in (mine, theirs))
    tiles = native.shape[0]
    swap = [(0, 1), (1, 0)]
    ahead = [(2 * i, 2 * i - 2) for i in range(1, pairs)] + [(2 * i + 1, 2 * i + 3) for i in range(pairs - 1)]
    ahead_across = [(2 * pairs * r + a, 2 * pairs * (1 - r) + b) for r in range(2) for a, b in ahead]
    first = [
        lax.ppermute(other_out, "par", swap),
        lax.ppermute(native_out, "row", swap),
        lax.ppermute(native_out, ("row", "pair", "par"), ahead_across),
        lax.ppermute(native, ("pair", "par"), ahead),
    ]
    piece = coupling_piece(place, quadrupoles, residuals.reshape(1, -1), shape)
    turns = rotations(piece, "pair")
    (relay, across, halo_across, halo), other, _ = lax.optimization_barrier((first, other, piece))
    half = BLOCK // 2
    cols = folded + shared
    sides = [piece[:, :half], piece[:, half:]]
    packed = [jnp.concatenate([a.reshape(-1, 128)] + sides) for a in (relay, other)]
    crossed = lax.ppermute(packed[0], "row", swap), lax.ppermute(packed[1], "par", swap)
    moved = native, across, halo, halo_across, turns, crossed
    native, across, halo, halo_across, turns, crossed = lax.optimization_barrier(moved)
    size = tiles * count
    second_across, second = (a[:size].reshape(native.shape) for a in crossed)
    own_by_row, own_by_par = ([a[size : size + cols][None], a[size + cols :][None]] for a in crossed)
    held = native, across, second, second_across, halo, halo_across

    column = jnp.stack(turns)
    by_row = lax.ppermute(column, "row", swap)
    by_par = lax.ppermute(column, "par", swap)
    held = jnp.concatenate(held)
    field = assemble(place, [held] + rotations(held, "mem"), (0, 1, 0, 1, 0, 1), rows, electrodes)

    sums = jnp.zeros((6 * tiles, 8, 128), jnp.float32)
    near = [(piece[None], 0, 0, 0, 0), (column, 0, 0, 0, 1)]
    staged = rows == 4
    if staged:
        sums = gradient_sums(place, field, sums, near, shape, window, False)
        by_row, by_par, sums = lax.optimization_barrier((by_row, by_par, sums))
    lower = jnp.concatenate([own_by_row[0], by_row[..., :half]])
    upper = jnp.concatenate([own_by_par[1], by_par[..., half:]])
    corner = lax.ppermute(lower, "par", swap), lax.ppermute(upper, "row", swap)
    beside = [
        [(own_by_row[0], 1, 0, 0, 0), (own_by_row[1], 1, 0, half, 0), (by_row, 1, 0, 0, 1)],
        [(own_by_par[0], 0, 1, 0, 0), (own_by_par[1], 0, 1, half, 0), (by_par, 0, 1, 0, 1)],
    ]
    if staged:
        for part in beside:
            sums = gradient_sums(place, field, sums, part, shape, window, False)
        corner, sums = lax.optimization_barrier((corner, sums))
    far = [(corner[0], 1, 1, 0, 0), (corner[1], 1, 1, half, 0)]
    part = far if staged else near + beside[0] + beside[1] + far
    sums = gradient_sums(place, field, sums, part, shape, window, True)

    sums = jnp.where(par == 0, sums, sums[::-1])
    sums = jnp.where(row == 0, sums, sums[:, ::-1])
    kept = jnp.where(par == 0, sums[:2], sums[2:])
    given = jnp.where(par == 0, sums[2:], sums[:2])
    total = kept + lax.ppermute(kept, "row", swap) + lax.ppermute(given, "par", swap)
    total = total + lax.ppermute(given, ("row", "par"), [(0, 3), (1, 2), (2, 1), (3, 0)])
    for turn in rotations(total, "mem"):
        total = total + turn
    return total * cell_weight


def solution(mesh):
    elec, space = mesh.devices.shape
    names = ("row", "mem", "pair", "par")
    finer = Mesh(mesh.devices.reshape(2, elec // 2, space // 2, 2), names)
    e, s = names[:2], names[2:]
    placed = (P(e, s, None, None), P(), P(), P(s, None, None))
    return jax.shard_map(local, mesh=finer, in_specs=placed, out_specs=P(s, None, None), check_vma=False)
```

```python
import jax
import jax.numpy as jnp
from jax import lax
from jax.experimental import pallas as pl
from jax.experimental.pallas import tpu as pltpu
from jax.sharding import Mesh, PartitionSpec as P

BLOCK = 256
CHUNK = 2048


def onehots(dest, first, rows, plus, minus, up, down):
    zero = jnp.zeros((16, CHUNK), jnp.bfloat16)
    for group in range(rows // 16):
        here = lax.broadcasted_iota(jnp.int16, (16, CHUNK), 0) + jnp.int16(16 * group)
        dest[pl.ds(first + 16 * group, 16)] = jnp.where(
            plus == here, up, jnp.where(minus == here, down, zero)
        )


def segment(kind, index, cols, electrodes):
    if kind == "folded":
        return BLOCK + index * cols
    at = index * cols
    return jnp.where(at < BLOCK, at, at - BLOCK + electrodes // 2)


def coupling_kernel(shape, place, quads, res, out, *hot):
    electrodes, rows, pairs, share, folded, shared = shape
    group = (2 * place[0] + place[3]) * pairs + place[2]
    row_base = (place[1] * rows + group // share) * BLOCK
    folded_base = row_base + segment("folded", group % share, folded, electrodes)
    shared_base = row_base + segment("shared", group % share, shared, electrodes)
    steps = quads.shape[1] // CHUNK

    def build(step, near_hot, far_hot, cols_hot, back_hot):
        at = pl.ds(pl.multiple_of(step * CHUNK, CHUNK), CHUNK)
        number = [quads[i : i + 1, at] for i in range(4)]
        empty = (number[0] == number[1]) | (number[2] == number[3])
        value = jnp.where(empty, 0.0, res[0:1, at])
        value = jnp.broadcast_to(value, (16, CHUNK)).astype(jnp.bfloat16)
        one = jnp.ones((16, CHUNK), jnp.bfloat16)

        def wide(row, base):
            local = (row - base) & (electrodes - 1)
            return jnp.broadcast_to(local, (16, CHUNK)).astype(jnp.int16)

        a, b, m, n = number
        onehots(near_hot, 0, BLOCK, wide(a, row_base), wide(b, row_base), one, -one)
        onehots(far_hot, 0, BLOCK, wide(m, row_base), wide(n, row_base), one, -one)
        onehots(cols_hot, 0, folded, wide(m, folded_base), wide(n, folded_base), value, -value)
        onehots(cols_hot, folded, shared, wide(m, shared_base), wide(n, shared_base), value, -value)
        onehots(back_hot, 0, folded, wide(a, folded_base), wide(b, folded_base), value, -value)

    def multiply(near_hot, far_hot, cols_hot, back_hot):
        dims = (((1,), (1,)), ((), ()))
        ahead = lax.dot_general(cols_hot[...], near_hot[...], dims, preferred_element_type=jnp.float32)
        back = lax.dot_general(back_hot[...], far_hot[...], dims, preferred_element_type=jnp.float32)
        return ahead[:folded] + back, ahead[folded:]

    def add(total, new):
        return total[0] + new[0], total[1] + new[1]

    build(0, *hot[:4])

    def pair(index, total):
        build(2 * index + 1, *hot[4:])
        total = add(total, multiply(*hot[:4]))
        build(jnp.minimum(2 * index + 2, steps - 1), *hot[:4])
        return add(total, multiply(*hot[4:]))

    zeros = jnp.zeros((folded, BLOCK), jnp.float32), jnp.zeros((shared, BLOCK), jnp.float32)
    total = lax.fori_loop(0, steps // 2, pair, zeros)
    out[:folded] = total[0].astype(jnp.bfloat16)
    out[folded:] = total[1].astype(jnp.bfloat16)


SMEM = pl.BlockSpec(memory_space=pltpu.SMEM)
VMEM = pl.BlockSpec(memory_space=pltpu.VMEM)


def coupling_piece(place, quadrupoles, residuals, shape):
    folded, shared = shape[4:]
    hot = [pltpu.VMEM((rows, CHUNK), jnp.bfloat16) for rows in (BLOCK, BLOCK, folded + shared, folded)]
    return pl.pallas_call(
        lambda *refs: coupling_kernel(shape, *refs),
        out_shape=jax.ShapeDtypeStruct((folded + shared, BLOCK), jnp.bfloat16),
        in_specs=[SMEM, VMEM, VMEM],
        out_specs=VMEM,
        scratch_shapes=hot + hot,
        compiler_params=pltpu.CompilerParams(vmem_limit_bytes=16 << 20),
        cost_estimate=pl.CostEstimate(
            flops=2 * (2 * folded + shared) * BLOCK * quadrupoles.shape[1],
            bytes_accessed=1 << 20,
            transcendentals=0,
        ),
        name="coupling_piece",
    )(place, quadrupoles, residuals)


def join_kernel(*refs):
    pieces, out = refs[:-1], refs[-1]
    tiles, count = out.shape[0] // len(pieces), out.shape[1]
    for slot, piece in enumerate(pieces):
        for tile in range(tiles):
            part = piece[tile] if len(piece.shape) == 3 else piece[count * tile : count * (tile + 1)]
            out[tiles * slot + tile] = part


def join(pieces):
    tiles, count, lanes = pieces[0].shape
    return pl.pallas_call(
        join_kernel,
        out_shape=jax.ShapeDtypeStruct((tiles * len(pieces), count, lanes), jnp.bfloat16),
        in_specs=[VMEM] * len(pieces),
        out_specs=VMEM,
        compiler_params=pltpu.CompilerParams(vmem_limit_bytes=16 << 20),
        cost_estimate=pl.CostEstimate(flops=0, bytes_accessed=1 << 10, transcendentals=0),
        name="join_pieces",
    )(*pieces)


def assemble_kernel(rows, far, place, *refs):
    pieces, field = refs[:-1], refs[-1]
    electrodes = field.shape[1]
    members = len(pieces)
    total, count, _ = pieces[0].shape
    tiles = total // len(far)
    for k, piece in enumerate(pieces):
        member = (place[1] + members - k) % members
        for slot, other in enumerate(far):
            row = 1 - place[0] if other else place[0]
            first = (row * members + member) * count - place[1] * rows * BLOCK
            first = pl.multiple_of((first + electrodes) % electrodes, count)
            for tile in range(tiles):
                field[tiles * (slot // 2) + tile, pl.ds(first, count)] = piece[tiles * slot + tile]


def assemble(place, pieces, far, rows, electrodes):
    return pl.pallas_call(
        lambda *refs: assemble_kernel(rows, far, *refs),
        out_shape=jax.ShapeDtypeStruct((pieces[0].shape[0] // 2, electrodes, 128), jnp.bfloat16),
        in_specs=[SMEM] + [VMEM] * len(pieces),
        out_specs=VMEM,
        compiler_params=pltpu.CompilerParams(vmem_limit_bytes=16 << 20),
        cost_estimate=pl.CostEstimate(flops=0, bytes_accessed=1 << 10, transcendentals=0),
        name="assemble_fields",
    )(place, *pieces)


def gradient_kernel(shape, parts, last, place, field, before, *refs):
    electrodes, rows, pairs, share, folded, shared = shape
    arrays = refs[: len(parts)]
    out, joined, turned, image = refs[len(parts) :]
    tiles = field.shape[0] // 3
    window = turned.shape[1]
    for kind, source, cols in (("folded", 0, folded), ("shared", folded, shared)):
        for array, (far_row, far_par, lane, turn) in zip(arrays, parts):
            row = 1 - place[0] if far_row else place[0]
            par = 1 - place[3] if far_par else place[3]
            for k in range(array.shape[0]):
                group = (2 * row + par) * pairs + (place[2] + pairs - turn - k) % pairs
                at = pl.multiple_of(segment(kind, group % share, cols, electrodes), 16)
                joined[pl.ds(at, cols), pl.ds(lane, array.shape[2])] = array[k, source : source + cols]
    first = pl.multiple_of((group // share) * BLOCK, BLOCK)
    turned[...] = joined[:window].T
    for tile in range(0, 3 * tiles, 2):
        two = [field[tile + i, pl.ds(first, window)] for i in range(2)]
        both = jnp.dot(turned[...], jnp.concatenate(two, axis=1), preferred_element_type=jnp.float32)
        image[tile] = both[:, :128]
        image[tile + 1] = both[:, 128:]
    lane = lax.broadcasted_iota(jnp.int32, (16, 128), 1)

    def fold(product):
        return product[:8] + product[8:]

    def along(value):
        return jnp.where(lane == 0, 0.0, value) - jnp.where(lane == 1, 0.0, pltpu.roll(value, 2, 1))

    nothing = jnp.zeros((1, 128), jnp.float32)
    for plane in range(2):

        def step(index, totals):
            at = pl.multiple_of(index * 16, 16)
            u = [
                field[tiles * plane + j, pl.ds(first + at, 16)].astype(jnp.float32)
                for j in range(2 * tiles)
            ]
            v = [image[tiles * plane + j, pl.ds(at, 16)] for j in range(2 * tiles)]
            new = []
            for j in range(tiles):
                new.append(fold(along(u[j]) * along(v[j])))
            for j in range(tiles - 1):
                new.append(fold((u[j] - u[j + 1]) * (v[j] - v[j + 1])))
            new.append(fold(u[tiles - 1] * v[tiles - 1]))
            for j in range(tiles):
                new.append(fold((u[j] - u[j + tiles]) * (v[j] - v[j + tiles])))
            return tuple(a + b for a, b in zip(totals, new))

        base = 3 * tiles * plane
        start = tuple(before[base + j] for j in range(3 * tiles))
        totals = lax.fori_loop(0, BLOCK // 16, step, start, unroll=8)
        if not last:
            for j in range(3 * tiles):
                out[base + j] = totals[j]
            continue
        total = [0.25 * jnp.sum(value, axis=0, keepdims=True) for value in totals]
        for j in range(tiles):
            out[2 * plane, 2 * j : 2 * j + 1] = pltpu.roll(total[j], 127, 1)
            out[2 * plane, 2 * j + 1 : 2 * j + 2] = total[tiles + j]
            out[2 * plane + 1, 2 * j : 2 * j + 1] = total[2 * tiles + j]
            out[2 * plane + 1, 2 * j + 1 : 2 * j + 2] = nothing


def gradient_sums(place, field, before, entries, shape, window, last):
    arrays = [entry[0] for entry in entries]
    parts = [entry[1:] for entry in entries]
    tiles = field.shape[0] // 3
    covered = max(window, BLOCK + shape[3] * shape[4])
    size = (4, 2 * tiles, 128) if last else before.shape
    return pl.pallas_call(
        lambda *refs: gradient_kernel(shape, parts, last, *refs),
        out_shape=jax.ShapeDtypeStruct(size, jnp.float32),
        in_specs=[SMEM, VMEM, VMEM] + [VMEM] * len(arrays),
        out_specs=VMEM,
        scratch_shapes=[
            pltpu.VMEM((covered, BLOCK), jnp.bfloat16),
            pltpu.VMEM((BLOCK, window), jnp.bfloat16),
            pltpu.VMEM((3 * tiles, BLOCK, 128), jnp.float32),
        ],
        compiler_params=pltpu.CompilerParams(vmem_limit_bytes=16 << 20),
        cost_estimate=pl.CostEstimate(
            flops=0, bytes_accessed=1 << 10, transcendentals=0
        ),
        name="gradient_sums",
    )(place, field, before, *arrays)


def rotations(value, axis):
    size = lax.axis_size(axis)
    return [
        lax.ppermute(value, axis, [(i, (i + k) % size) for i in range(size)]) for k in range(1, size)
    ]


def local(potentials, quadrupoles, residuals, cell_weight):
    count = potentials.shape[0]
    row, mem = lax.axis_index("row"), lax.axis_index("mem")
    pair, par = lax.axis_index("pair"), lax.axis_index("par")
    members, pairs = lax.axis_size("mem"), lax.axis_size("pair")
    electrodes = 2 * members * count
    rows = electrodes // BLOCK // members
    window = electrodes // 2 + BLOCK
    share = 4 * pairs // rows
    folded = -(-(window - 2 * BLOCK) // (16 * share)) * 16
    shared = 2 * BLOCK // share
    shape = (electrodes, rows, pairs, share, folded, shared)
    place = jnp.stack([row, mem, pair, par]).astype(jnp.int32)

    planes = jnp.transpose(potentials, (1, 2, 0, 3))
    even, odd = planes[:, 0::2], planes[:, ::-1][:, 0::2]
    mine = jnp.where(row == 0, even, odd)
    theirs = jnp.where(row == 0, odd, even)
    native, native_out = (jnp.where(par == 0, a[0], a[1]) for a in (mine, theirs))
    other, other_out = (jnp.where(par == 0, a[1], a[0]) for a in (mine, theirs))
    tiles = native.shape[0]
    swap = [(0, 1), (1, 0)]
    ahead = [(2 * i, 2 * i - 2) for i in range(1, pairs)] + [(2 * i + 1, 2 * i + 3) for i in range(pairs - 1)]
    ahead_across = [(2 * pairs * r + a, 2 * pairs * (1 - r) + b) for r in range(2) for a, b in ahead]
    first = [
        lax.ppermute(other_out, "par", swap),
        lax.ppermute(native_out, "row", swap),
        lax.ppermute(native_out, ("row", "pair", "par"), ahead_across),
        lax.ppermute(native, ("pair", "par"), ahead),
    ]
    piece = coupling_piece(place, quadrupoles, residuals.reshape(1, -1), shape)
    turns = rotations(piece, "pair")
    (relay, across, halo_across, halo), other, _ = lax.optimization_barrier((first, other, piece))
    half = BLOCK // 2
    cols = folded + shared
    sides = [piece[:, :half], piece[:, half:]]
    packed = [jnp.concatenate([a.reshape(-1, 128)] + sides) for a in (relay, other)]
    crossed = lax.ppermute(packed[0], "row", swap), lax.ppermute(packed[1], "par", swap)
    moved = native, across, halo, halo_across, turns, crossed
    native, across, halo, halo_across, _, crossed = lax.optimization_barrier(moved)
    size = tiles * count
    own_by_row, own_by_par = ([a[size : size + cols][None], a[size + cols :][None]] for a in crossed)
    column = jnp.stack(turns)
    by_row = lax.ppermute(column, "row", swap)
    by_par = lax.ppermute(column, "par", swap)
    held = join([native, across, crossed[1], crossed[0], halo, halo_across])
    field = assemble(place, [held] + rotations(held, "mem"), (0, 1, 0, 1, 0, 1), rows, electrodes)

    sums = jnp.zeros((6 * tiles, 8, 128), jnp.float32)
    near = [(piece[None], 0, 0, 0, 0), (column, 0, 0, 0, 1)]
    staged = rows == 4
    if staged:
        sums = gradient_sums(place, field, sums, near, shape, window, False)
        by_row, by_par, sums = lax.optimization_barrier((by_row, by_par, sums))
    lower = jnp.concatenate([own_by_row[0], by_row[..., :half]])
    upper = jnp.concatenate([own_by_par[1], by_par[..., half:]])
    corner = lax.ppermute(lower, "par", swap), lax.ppermute(upper, "row", swap)
    beside = [
        [(own_by_row[0], 1, 0, 0, 0), (own_by_row[1], 1, 0, half, 0), (by_row, 1, 0, 0, 1)],
        [(own_by_par[0], 0, 1, 0, 0), (own_by_par[1], 0, 1, half, 0), (by_par, 0, 1, 0, 1)],
    ]
    if staged:
        for part in beside:
            sums = gradient_sums(place, field, sums, part, shape, window, False)
        corner, sums = lax.optimization_barrier((corner, sums))
    far = [(corner[0], 1, 1, 0, 0), (corner[1], 1, 1, half, 0)]
    part = far if staged else near + beside[0] + beside[1] + far
    sums = gradient_sums(place, field, sums, part, shape, window, True)

    sums = jnp.where(par == 0, sums, sums[::-1])
    sums = jnp.where(row == 0, sums, sums[:, ::-1])
    kept = jnp.where(par == 0, sums[:2], sums[2:])
    given = jnp.where(par == 0, sums[2:], sums[:2])
    total = kept + lax.ppermute(kept, "row", swap) + lax.ppermute(given, "par", swap)
    total = total + lax.ppermute(given, ("row", "par"), [(0, 3), (1, 2), (2, 1), (3, 0)])
    for turn in rotations(total, "mem"):
        total = total + turn
    return total * cell_weight


def solution(mesh):
    elec, space = mesh.devices.shape
    names = ("row", "mem", "pair", "par")
    finer = Mesh(mesh.devices.reshape(2, elec // 2, space // 2, 2), names)
    e, s = names[:2], names[2:]
    placed = (P(e, s, None, None), P(), P(), P(s, None, None))
    return jax.shard_map(local, mesh=finer, in_specs=placed, out_specs=P(s, None, None), check_vma=False)
```

```python
import jax
import jax.numpy as jnp
from jax import lax
from jax.experimental import pallas as pl
from jax.experimental.pallas import tpu as pltpu
from jax.sharding import Mesh, PartitionSpec as P

BLOCK = 256
CHUNK = 4096


def onehots(dest, first, rows, plus, minus, up, down):
    zero = jnp.zeros((16, CHUNK), jnp.bfloat16)
    for group in range(rows // 16):
        here = lax.broadcasted_iota(jnp.int16, (16, CHUNK), 0) + jnp.int16(16 * group)
        dest[pl.ds(first + 16 * group, 16)] = jnp.where(
            plus == here, up, jnp.where(minus == here, down, zero)
        )


def segment(kind, index, cols, electrodes):
    if kind == "folded":
        return BLOCK + index * cols
    at = index * cols
    return jnp.where(at < BLOCK, at, at - BLOCK + electrodes // 2)


def coupling_kernel(shape, place, quads, res, out, *hot):
    electrodes, rows, pairs, share, folded, shared = shape
    group = (2 * place[0] + place[3]) * pairs + place[2]
    row_base = (place[1] * rows + group // share) * BLOCK
    folded_base = row_base + segment("folded", group % share, folded, electrodes)
    shared_base = row_base + segment("shared", group % share, shared, electrodes)
    steps = quads.shape[1] // CHUNK

    def build(step, near_hot, far_hot, cols_hot, back_hot):
        at = pl.ds(pl.multiple_of(step * CHUNK, CHUNK), CHUNK)
        number = [quads[i : i + 1, at] for i in range(4)]
        empty = (number[0] == number[1]) | (number[2] == number[3])
        value = jnp.where(empty, 0.0, res[0:1, at])
        value = jnp.broadcast_to(value, (16, CHUNK)).astype(jnp.bfloat16)
        one = jnp.ones((16, CHUNK), jnp.bfloat16)

        def wide(row, base):
            local = (row - base) & (electrodes - 1)
            return jnp.broadcast_to(local, (16, CHUNK)).astype(jnp.int16)

        a, b, m, n = number
        onehots(near_hot, 0, BLOCK, wide(a, row_base), wide(b, row_base), one, -one)
        onehots(far_hot, 0, BLOCK, wide(m, row_base), wide(n, row_base), one, -one)
        onehots(cols_hot, 0, folded, wide(m, folded_base), wide(n, folded_base), value, -value)
        onehots(cols_hot, folded, shared, wide(m, shared_base), wide(n, shared_base), value, -value)
        onehots(back_hot, 0, folded, wide(a, folded_base), wide(b, folded_base), value, -value)

    def multiply(near_hot, far_hot, cols_hot, back_hot):
        dims = (((1,), (1,)), ((), ()))
        ahead = lax.dot_general(cols_hot[...], near_hot[...], dims, preferred_element_type=jnp.float32)
        back = lax.dot_general(back_hot[...], far_hot[...], dims, preferred_element_type=jnp.float32)
        return ahead[:folded] + back, ahead[folded:]

    def add(total, new):
        return total[0] + new[0], total[1] + new[1]

    build(0, *hot[:4])

    def pair(index, total):
        build(2 * index + 1, *hot[4:])
        total = add(total, multiply(*hot[:4]))
        build(jnp.minimum(2 * index + 2, steps - 1), *hot[:4])
        return add(total, multiply(*hot[4:]))

    zeros = jnp.zeros((folded, BLOCK), jnp.float32), jnp.zeros((shared, BLOCK), jnp.float32)
    total = lax.fori_loop(0, steps // 2, pair, zeros)
    out[:folded] = total[0].astype(jnp.bfloat16)
    out[folded:] = total[1].astype(jnp.bfloat16)


SMEM = pl.BlockSpec(memory_space=pltpu.SMEM)
VMEM = pl.BlockSpec(memory_space=pltpu.VMEM)


def coupling_piece(place, quadrupoles, residuals, shape):
    folded, shared = shape[4:]
    hot = [pltpu.VMEM((rows, CHUNK), jnp.bfloat16) for rows in (BLOCK, BLOCK, folded + shared, folded)]
    return pl.pallas_call(
        lambda *refs: coupling_kernel(shape, *refs),
        out_shape=jax.ShapeDtypeStruct((folded + shared, BLOCK), jnp.bfloat16),
        in_specs=[SMEM, VMEM, VMEM],
        out_specs=VMEM,
        scratch_shapes=hot + hot,
        compiler_params=pltpu.CompilerParams(vmem_limit_bytes=28 << 20),
        cost_estimate=pl.CostEstimate(
            flops=2 * (2 * folded + shared) * BLOCK * quadrupoles.shape[1],
            bytes_accessed=1 << 20,
            transcendentals=0,
        ),
        name="coupling_piece",
    )(place, quadrupoles, residuals)


def join_kernel(*refs):
    pieces, out = refs[:-1], refs[-1]
    tiles = pieces[0].shape[0]
    for slot, piece in enumerate(pieces):
        for tile in range(tiles):
            out[tiles * slot + tile] = piece[tile]


def join(pieces):
    tiles, count, lanes = pieces[0].shape
    return pl.pallas_call(
        join_kernel,
        out_shape=jax.ShapeDtypeStruct((tiles * len(pieces), count, lanes), jnp.bfloat16),
        in_specs=[VMEM] * len(pieces),
        out_specs=VMEM,
        compiler_params=pltpu.CompilerParams(vmem_limit_bytes=16 << 20),
        cost_estimate=pl.CostEstimate(flops=0, bytes_accessed=1 << 10, transcendentals=0),
        name="join_pieces",
    )(*pieces)


def assemble_kernel(rows, tiles, groups, place, *refs):
    pieces, field = refs[:-1], refs[-1]
    electrodes = field.shape[1]
    members = len(pieces) // len(groups)
    count = pieces[0].shape[1]
    for index, piece in enumerate(pieces):
        k = index % members
        member = (place[1] + members - k) % members
        for position, (slot, other) in enumerate(groups[index // members]):
            row = 1 - place[0] if other else place[0]
            first = (row * members + member) * count - place[1] * rows * BLOCK
            first = pl.multiple_of((first + electrodes) % electrodes, count)
            for tile in range(tiles):
                field[tiles * slot + tile, pl.ds(first, count)] = piece[tiles * position + tile]


def assemble(place, pieces, groups, tiles, rows, electrodes):
    return pl.pallas_call(
        lambda *refs: assemble_kernel(rows, tiles, groups, *refs),
        out_shape=jax.ShapeDtypeStruct((3 * tiles, electrodes, 128), jnp.bfloat16),
        in_specs=[SMEM] + [VMEM] * len(pieces),
        out_specs=VMEM,
        compiler_params=pltpu.CompilerParams(vmem_limit_bytes=16 << 20),
        cost_estimate=pl.CostEstimate(flops=0, bytes_accessed=1 << 10, transcendentals=0),
        name="assemble_fields",
    )(place, *pieces)


def gradient_kernel(shape, parts, last, place, field, before, *refs):
    electrodes, rows, pairs, share, folded, shared = shape
    arrays = refs[: len(parts)]
    out, joined, turned, image = refs[len(parts) :]
    tiles = field.shape[0] // 3
    window = turned.shape[1]
    for kind, source, cols in (("folded", 0, folded), ("shared", folded, shared)):
        for array, (far_row, far_par, lane, turn) in zip(arrays, parts):
            row = 1 - place[0] if far_row else place[0]
            par = 1 - place[3] if far_par else place[3]
            for k in range(array.shape[0]):
                group = (2 * row + par) * pairs + (place[2] + pairs - turn - k) % pairs
                at = pl.multiple_of(segment(kind, group % share, cols, electrodes), 16)
                joined[pl.ds(at, cols), pl.ds(lane, array.shape[2])] = array[k, source : source + cols]
    first = pl.multiple_of((group // share) * BLOCK, BLOCK)
    turned[...] = joined[:window].T
    for tile in range(0, 3 * tiles, 2):
        two = [field[tile + i, pl.ds(first, window)] for i in range(2)]
        both = jnp.dot(turned[...], jnp.concatenate(two, axis=1), preferred_element_type=jnp.float32)
        image[tile] = both[:, :128]
        image[tile + 1] = both[:, 128:]
    lane = lax.broadcasted_iota(jnp.int32, (16, 128), 1)

    def fold(product):
        return product[:8] + product[8:]

    def along(value):
        return jnp.where(lane == 0, 0.0, value) - jnp.where(lane == 1, 0.0, pltpu.roll(value, 2, 1))

    nothing = jnp.zeros((1, 128), jnp.float32)
    for plane in range(2):

        def step(index, totals):
            at = pl.multiple_of(index * 16, 16)
            u = [
                field[tiles * plane + j, pl.ds(first + at, 16)].astype(jnp.float32)
                for j in range(2 * tiles)
            ]
            v = [image[tiles * plane + j, pl.ds(at, 16)] for j in range(2 * tiles)]
            new = []
            for j in range(tiles):
                new.append(fold(along(u[j]) * along(v[j])))
            for j in range(tiles - 1):
                new.append(fold((u[j] - u[j + 1]) * (v[j] - v[j + 1])))
            new.append(fold(u[tiles - 1] * v[tiles - 1]))
            for j in range(tiles):
                new.append(fold((u[j] - u[j + tiles]) * (v[j] - v[j + tiles])))
            return tuple(a + b for a, b in zip(totals, new))

        base = 3 * tiles * plane
        start = tuple(before[base + j] for j in range(3 * tiles))
        totals = lax.fori_loop(0, BLOCK // 16, step, start, unroll=8)
        if not last:
            for j in range(3 * tiles):
                out[base + j] = totals[j]
            continue
        total = [0.25 * jnp.sum(value, axis=0, keepdims=True) for value in totals]
        for j in range(tiles):
            out[2 * plane, 2 * j : 2 * j + 1] = pltpu.roll(total[j], 127, 1)
            out[2 * plane, 2 * j + 1 : 2 * j + 2] = total[tiles + j]
            out[2 * plane + 1, 2 * j : 2 * j + 1] = total[2 * tiles + j]
            out[2 * plane + 1, 2 * j + 1 : 2 * j + 2] = nothing


def gradient_sums(place, field, before, entries, shape, window, last):
    arrays = [entry[0] for entry in entries]
    parts = [entry[1:] for entry in entries]
    tiles = field.shape[0] // 3
    covered = max(window, BLOCK + shape[3] * shape[4])
    size = (4, 2 * tiles, 128) if last else before.shape
    return pl.pallas_call(
        lambda *refs: gradient_kernel(shape, parts, last, *refs),
        out_shape=jax.ShapeDtypeStruct(size, jnp.float32),
        in_specs=[SMEM, VMEM, VMEM] + [VMEM] * len(arrays),
        out_specs=VMEM,
        scratch_shapes=[
            pltpu.VMEM((covered, BLOCK), jnp.bfloat16),
            pltpu.VMEM((BLOCK, window), jnp.bfloat16),
            pltpu.VMEM((3 * tiles, BLOCK, 128), jnp.float32),
        ],
        compiler_params=pltpu.CompilerParams(vmem_limit_bytes=16 << 20),
        cost_estimate=pl.CostEstimate(
            flops=0, bytes_accessed=1 << 10, transcendentals=0
        ),
        name="gradient_sums",
    )(place, field, before, *arrays)


def rotations(value, axis):
    size = lax.axis_size(axis)
    return [
        lax.ppermute(value, axis, [(i, (i + k) % size) for i in range(size)]) for k in range(1, size)
    ]


def local(potentials, quadrupoles, residuals, cell_weight):
    count = potentials.shape[0]
    row, mem = lax.axis_index("row"), lax.axis_index("mem")
    pair, par = lax.axis_index("pair"), lax.axis_index("par")
    members, pairs = lax.axis_size("mem"), lax.axis_size("pair")
    electrodes = 2 * members * count
    rows = electrodes // BLOCK // members
    window = electrodes // 2 + BLOCK
    share = 4 * pairs // rows
    folded = -(-(window - 2 * BLOCK) // (16 * share)) * 16
    shared = 2 * BLOCK // share
    shape = (electrodes, rows, pairs, share, folded, shared)
    place = jnp.stack([row, mem, pair, par]).astype(jnp.int32)

    planes = jnp.transpose(potentials, (1, 2, 0, 3))
    even, odd = planes[:, 0::2], planes[:, ::-1][:, 0::2]
    mine = jnp.where(row == 0, even, odd)
    theirs = jnp.where(row == 0, odd, even)
    native, native_out = (jnp.where(par == 0, a[0], a[1]) for a in (mine, theirs))
    other, other_out = (jnp.where(par == 0, a[1], a[0]) for a in (mine, theirs))
    tiles = native.shape[0]
    swap = [(0, 1), (1, 0)]
    ahead = [(2 * i, 2 * i - 2) for i in range(1, pairs)] + [(2 * i + 1, 2 * i + 3) for i in range(pairs - 1)]
    first = [
        lax.ppermute(native_out, "row", swap),
        lax.ppermute(other_out, ("row", "par"), [(0, 3), (1, 2), (2, 1), (3, 0)]),
        lax.ppermute(other, "par", swap),
        lax.ppermute(native, ("pair", "par"), ahead),
    ]
    piece = coupling_piece(place, quadrupoles, residuals.reshape(1, -1), shape)
    turns = rotations(piece, "pair")
    own = piece[None]
    own_by_row, own_by_par = lax.ppermute(own, "row", swap), lax.ppermute(own, "par", swap)
    first, _ = lax.optimization_barrier((first, piece))
    column = jnp.stack(turns)
    by_row = lax.ppermute(column, "row", swap)
    by_par = lax.ppermute(column, "par", swap)

    moved = first, native, turns, own_by_row, own_by_par
    first, native, _, own_by_row, own_by_par = lax.optimization_barrier(moved)
    across, second_across, second, halo = first
    halo_across = lax.ppermute(across, ("pair", "par"), ahead)
    held = join([native, across, second, second_across, halo])
    pieces = [held] + rotations(held, "mem") + [halo_across] + rotations(halo_across, "mem")
    groups = ((0, 0), (0, 1), (1, 0), (1, 1), (2, 0)), ((2, 1),)
    field = assemble(place, pieces, groups, tiles, rows, electrodes)

    sums = jnp.zeros((6 * tiles, 8, 128), jnp.float32)
    half = BLOCK // 2
    near = [(own, 0, 0, 0, 0), (column, 0, 0, 0, 1)]
    staged = rows == 4
    if staged:
        sums = gradient_sums(place, field, sums, near, shape, window, False)
    lower = jnp.concatenate([own_by_row[..., :half], by_row[..., :half]])
    upper = jnp.concatenate([own_by_par[..., half:], by_par[..., half:]])
    corner = lax.ppermute(lower, "par", swap), lax.ppermute(upper, "row", swap)
    beside = [
        [(own_by_row, 1, 0, 0, 0), (by_row, 1, 0, 0, 1)],
        [(own_by_par, 0, 1, 0, 0), (by_par, 0, 1, 0, 1)],
    ]
    if staged:
        for part in beside:
            sums = gradient_sums(place, field, sums, part, shape, window, False)
        corner, sums = lax.optimization_barrier((corner, sums))
    far = [(corner[0], 1, 1, 0, 0), (corner[1], 1, 1, half, 0)]
    part = far if staged else near + beside[0] + beside[1] + far
    sums = gradient_sums(place, field, sums, part, shape, window, True)

    sums = jnp.where(par == 0, sums, sums[::-1])
    sums = jnp.where(row == 0, sums, sums[:, ::-1])
    kept = jnp.where(par == 0, sums[:2], sums[2:])
    given = jnp.where(par == 0, sums[2:], sums[:2])
    total = kept + lax.ppermute(kept, "row", swap) + lax.ppermute(given, "par", swap)
    total = total + lax.ppermute(given, ("row", "par"), [(0, 3), (1, 2), (2, 1), (3, 0)])
    for turn in rotations(total, "mem"):
        total = total + turn
    return total * cell_weight


def solution(mesh):
    elec, space = mesh.devices.shape
    names = ("row", "mem", "pair", "par")
    finer = Mesh(mesh.devices.reshape(2, elec // 2, space // 2, 2), names)
    e, s = names[:2], names[2:]
    placed = (P(e, s, None, None), P(), P(), P(s, None, None))
    return jax.shard_map(local, mesh=finer, in_specs=placed, out_specs=P(s, None, None), check_vma=False)
```

```python
import jax
import jax.numpy as jnp
from jax import lax
from jax.experimental import pallas as pl
from jax.experimental.pallas import tpu as pltpu
from jax.sharding import Mesh, PartitionSpec as P

BLOCK = 256
CHUNK = 4096


def onehots(dest, first, rows, plus, minus, up, down):
    zero = jnp.zeros((16, CHUNK), jnp.bfloat16)
    for group in range(rows // 16):
        here = lax.broadcasted_iota(jnp.int16, (16, CHUNK), 0) + jnp.int16(16 * group)
        dest[pl.ds(first + 16 * group, 16)] = jnp.where(
            plus == here, up, jnp.where(minus == here, down, zero)
        )


def segment(kind, index, cols, electrodes):
    if kind == "folded":
        return BLOCK + index * cols
    at = index * cols
    return jnp.where(at < BLOCK, at, at - BLOCK + electrodes // 2)


def coupling_kernel(shape, place, quads, res, out, *hot):
    electrodes, rows, pairs, share, folded, shared = shape
    group = (2 * place[0] + place[3]) * pairs + place[2]
    row_base = (place[1] * rows + group // share) * BLOCK
    folded_base = row_base + segment("folded", group % share, folded, electrodes)
    shared_base = row_base + segment("shared", group % share, shared, electrodes)
    steps = quads.shape[1] // CHUNK

    def build(step, near_hot, far_hot, cols_hot, back_hot):
        at = pl.ds(pl.multiple_of(step * CHUNK, CHUNK), CHUNK)
        number = [quads[i : i + 1, at] for i in range(4)]
        empty = (number[0] == number[1]) | (number[2] == number[3])
        value = jnp.where(empty, 0.0, res[0:1, at])
        value = jnp.broadcast_to(value, (16, CHUNK)).astype(jnp.bfloat16)
        one = jnp.ones((16, CHUNK), jnp.bfloat16)

        def wide(row, base):
            local = (row - base) & (electrodes - 1)
            return jnp.broadcast_to(local, (16, CHUNK)).astype(jnp.int16)

        a, b, m, n = number
        onehots(near_hot, 0, BLOCK, wide(a, row_base), wide(b, row_base), one, -one)
        onehots(far_hot, 0, BLOCK, wide(m, row_base), wide(n, row_base), one, -one)
        onehots(cols_hot, 0, folded, wide(m, folded_base), wide(n, folded_base), value, -value)
        onehots(cols_hot, folded, shared, wide(m, shared_base), wide(n, shared_base), value, -value)
        onehots(back_hot, 0, folded, wide(a, folded_base), wide(b, folded_base), value, -value)

    def multiply(near_hot, far_hot, cols_hot, back_hot):
        dims = (((1,), (1,)), ((), ()))
        ahead = lax.dot_general(cols_hot[...], near_hot[...], dims, preferred_element_type=jnp.float32)
        back = lax.dot_general(back_hot[...], far_hot[...], dims, preferred_element_type=jnp.float32)
        return ahead[:folded] + back, ahead[folded:]

    def add(total, new):
        return total[0] + new[0], total[1] + new[1]

    build(0, *hot[:4])

    def pair(index, total):
        build(2 * index + 1, *hot[4:])
        total = add(total, multiply(*hot[:4]))
        build(jnp.minimum(2 * index + 2, steps - 1), *hot[:4])
        return add(total, multiply(*hot[4:]))

    zeros = jnp.zeros((folded, BLOCK), jnp.float32), jnp.zeros((shared, BLOCK), jnp.float32)
    total = lax.fori_loop(0, steps // 2, pair, zeros)
    out[:folded] = total[0].astype(jnp.bfloat16)
    out[folded:] = total[1].astype(jnp.bfloat16)


SMEM = pl.BlockSpec(memory_space=pltpu.SMEM)
VMEM = pl.BlockSpec(memory_space=pltpu.VMEM)


def coupling_piece(place, quadrupoles, residuals, shape):
    folded, shared = shape[4:]
    hot = [pltpu.VMEM((rows, CHUNK), jnp.bfloat16) for rows in (BLOCK, BLOCK, folded + shared, folded)]
    return pl.pallas_call(
        lambda *refs: coupling_kernel(shape, *refs),
        out_shape=jax.ShapeDtypeStruct((folded + shared, BLOCK), jnp.bfloat16),
        in_specs=[SMEM, VMEM, VMEM],
        out_specs=VMEM,
        scratch_shapes=hot + hot,
        compiler_params=pltpu.CompilerParams(vmem_limit_bytes=28 << 20),
        cost_estimate=pl.CostEstimate(
            flops=2 * (2 * folded + shared) * BLOCK * quadrupoles.shape[1],
            bytes_accessed=1 << 20,
            transcendentals=0,
        ),
        name="coupling_piece",
    )(place, quadrupoles, residuals)


def join_kernel(*refs):
    pieces, out = refs[:-1], refs[-1]
    tiles = pieces[0].shape[0]
    for slot, piece in enumerate(pieces):
        for tile in range(tiles):
            out[tiles * slot + tile] = piece[tile]


def join(pieces):
    tiles, count, lanes = pieces[0].shape
    return pl.pallas_call(
        join_kernel,
        out_shape=jax.ShapeDtypeStruct((tiles * len(pieces), count, lanes), jnp.bfloat16),
        in_specs=[VMEM] * len(pieces),
        out_specs=VMEM,
        compiler_params=pltpu.CompilerParams(vmem_limit_bytes=16 << 20),
        cost_estimate=pl.CostEstimate(flops=0, bytes_accessed=1 << 10, transcendentals=0),
        name="join_pieces",
    )(*pieces)


def assemble_kernel(rows, tiles, groups, place, *refs):
    pieces, field = refs[:-1], refs[-1]
    electrodes = field.shape[1]
    members = len(pieces) // len(groups)
    count = pieces[0].shape[1]
    for index, piece in enumerate(pieces):
        k = index % members
        member = (place[1] + members - k) % members
        for position, (slot, other) in enumerate(groups[index // members]):
            row = 1 - place[0] if other else place[0]
            first = (row * members + member) * count - place[1] * rows * BLOCK
            first = pl.multiple_of((first + electrodes) % electrodes, count)
            for tile in range(tiles):
                field[tiles * slot + tile, pl.ds(first, count)] = piece[tiles * position + tile]


def assemble(place, pieces, groups, tiles, rows, electrodes):
    return pl.pallas_call(
        lambda *refs: assemble_kernel(rows, tiles, groups, *refs),
        out_shape=jax.ShapeDtypeStruct((3 * tiles, electrodes, 128), jnp.bfloat16),
        in_specs=[SMEM] + [VMEM] * len(pieces),
        out_specs=VMEM,
        compiler_params=pltpu.CompilerParams(vmem_limit_bytes=16 << 20),
        cost_estimate=pl.CostEstimate(flops=0, bytes_accessed=1 << 10, transcendentals=0),
        name="assemble_fields",
    )(place, *pieces)


def gradient_kernel(shape, parts, last, place, field, before, *refs):
    electrodes, rows, pairs, share, folded, shared = shape
    arrays = refs[: len(parts)]
    out, joined, turned, image = refs[len(parts) :]
    tiles = field.shape[0] // 3
    window = turned.shape[1]
    for kind, source, cols in (("folded", 0, folded), ("shared", folded, shared)):
        for array, (far_row, far_par, lane, turn) in zip(arrays, parts):
            row = 1 - place[0] if far_row else place[0]
            par = 1 - place[3] if far_par else place[3]
            for k in range(array.shape[0]):
                group = (2 * row + par) * pairs + (place[2] + pairs - turn - k) % pairs
                at = pl.multiple_of(segment(kind, group % share, cols, electrodes), 16)
                joined[pl.ds(at, cols), pl.ds(lane, array.shape[2])] = array[k, source : source + cols]
    first = pl.multiple_of((group // share) * BLOCK, BLOCK)
    turned[...] = joined[:window].T
    for tile in range(0, 3 * tiles, 2):
        two = [field[tile + i, pl.ds(first, window)] for i in range(2)]
        both = jnp.dot(turned[...], jnp.concatenate(two, axis=1), preferred_element_type=jnp.float32)
        image[tile] = both[:, :128]
        image[tile + 1] = both[:, 128:]
    lane = lax.broadcasted_iota(jnp.int32, (16, 128), 1)

    def fold(product):
        return product[:8] + product[8:]

    def along(value):
        return jnp.where(lane == 0, 0.0, value) - jnp.where(lane == 1, 0.0, pltpu.roll(value, 2, 1))

    nothing = jnp.zeros((1, 128), jnp.float32)
    for plane in range(2):

        def step(index, totals):
            at = pl.multiple_of(index * 16, 16)
            u = [
                field[tiles * plane + j, pl.ds(first + at, 16)].astype(jnp.float32)
                for j in range(2 * tiles)
            ]
            v = [image[tiles * plane + j, pl.ds(at, 16)] for j in range(2 * tiles)]
            new = []
            for j in range(tiles):
                new.append(fold(along(u[j]) * along(v[j])))
            for j in range(tiles - 1):
                new.append(fold((u[j] - u[j + 1]) * (v[j] - v[j + 1])))
            new.append(fold(u[tiles - 1] * v[tiles - 1]))
            for j in range(tiles):
                new.append(fold((u[j] - u[j + tiles]) * (v[j] - v[j + tiles])))
            return tuple(a + b for a, b in zip(totals, new))

        base = 3 * tiles * plane
        start = tuple(before[base + j] for j in range(3 * tiles))
        totals = lax.fori_loop(0, BLOCK // 16, step, start, unroll=8)
        if not last:
            for j in range(3 * tiles):
                out[base + j] = totals[j]
            continue
        total = [0.25 * jnp.sum(value, axis=0, keepdims=True) for value in totals]
        for j in range(tiles):
            out[2 * plane, 2 * j : 2 * j + 1] = pltpu.roll(total[j], 127, 1)
            out[2 * plane, 2 * j + 1 : 2 * j + 2] = total[tiles + j]
            out[2 * plane + 1, 2 * j : 2 * j + 1] = total[2 * tiles + j]
            out[2 * plane + 1, 2 * j + 1 : 2 * j + 2] = nothing


def gradient_sums(place, field, before, entries, shape, window, last):
    arrays = [entry[0] for entry in entries]
    parts = [entry[1:] for entry in entries]
    tiles = field.shape[0] // 3
    covered = max(window, BLOCK + shape[3] * shape[4])
    size = (4, 2 * tiles, 128) if last else before.shape
    return pl.pallas_call(
        lambda *refs: gradient_kernel(shape, parts, last, *refs),
        out_shape=jax.ShapeDtypeStruct(size, jnp.float32),
        in_specs=[SMEM, VMEM, VMEM] + [VMEM] * len(arrays),
        out_specs=VMEM,
        scratch_shapes=[
            pltpu.VMEM((covered, BLOCK), jnp.bfloat16),
            pltpu.VMEM((BLOCK, window), jnp.bfloat16),
            pltpu.VMEM((3 * tiles, BLOCK, 128), jnp.float32),
        ],
        compiler_params=pltpu.CompilerParams(vmem_limit_bytes=16 << 20),
        cost_estimate=pl.CostEstimate(
            flops=0, bytes_accessed=1 << 10, transcendentals=0
        ),
        name="gradient_sums",
    )(place, field, before, *arrays)


def rotations(value, axis):
    size = lax.axis_size(axis)
    return [
        lax.ppermute(value, axis, [(i, (i + k) % size) for i in range(size)]) for k in range(1, size)
    ]


def local(potentials, quadrupoles, residuals, cell_weight):
    count = potentials.shape[0]
    row, mem = lax.axis_index("row"), lax.axis_index("mem")
    pair, par = lax.axis_index("pair"), lax.axis_index("par")
    members, pairs = lax.axis_size("mem"), lax.axis_size("pair")
    electrodes = 2 * members * count
    rows = electrodes // BLOCK // members
    window = electrodes // 2 + BLOCK
    share = 4 * pairs // rows
    folded = -(-(window - 2 * BLOCK) // (16 * share)) * 16
    shared = 2 * BLOCK // share
    shape = (electrodes, rows, pairs, share, folded, shared)
    place = jnp.stack([row, mem, pair, par]).astype(jnp.int32)

    planes = jnp.transpose(potentials, (1, 2, 0, 3))
    even, odd = planes[:, 0::2], planes[:, ::-1][:, 0::2]
    mine = jnp.where(row == 0, even, odd)
    theirs = jnp.where(row == 0, odd, even)
    native, native_out = (jnp.where(par == 0, a[0], a[1]) for a in (mine, theirs))
    other, other_out = (jnp.where(par == 0, a[1], a[0]) for a in (mine, theirs))
    tiles = native.shape[0]
    swap = [(0, 1), (1, 0)]
    ahead = [(2 * i, 2 * i - 2) for i in range(1, pairs)] + [(2 * i + 1, 2 * i + 3) for i in range(pairs - 1)]
    first = [
        lax.ppermute(native_out, "row", swap),
        lax.ppermute(other_out, ("row", "par"), [(0, 3), (1, 2), (2, 1), (3, 0)]),
        lax.ppermute(other, "par", swap),
        lax.ppermute(native, ("pair", "par"), ahead),
    ]
    piece = coupling_piece(place, quadrupoles, residuals.reshape(1, -1), shape)
    turns = rotations(piece, "pair")
    first, own = lax.optimization_barrier((first, piece[None]))
    own_by_row, own_by_par = lax.ppermute(own, "row", swap), lax.ppermute(own, "par", swap)
    column = jnp.stack(turns)
    by_row = lax.ppermute(column, "row", swap)
    by_par = lax.ppermute(column, "par", swap)

    moved = first, native, turns, own_by_row, own_by_par
    first, native, _, own_by_row, own_by_par = lax.optimization_barrier(moved)
    across, second_across, second, halo = first
    halo_across = lax.ppermute(across, ("pair", "par"), ahead)
    halo_across, _ = lax.optimization_barrier((halo_across, (by_row, by_par)))
    held = join([native, across, second, second_across, halo])
    pieces = [held] + rotations(held, "mem") + [halo_across] + rotations(halo_across, "mem")
    groups = ((0, 0), (0, 1), (1, 0), (1, 1), (2, 0)), ((2, 1),)
    field = assemble(place, pieces, groups, tiles, rows, electrodes)

    sums = jnp.zeros((6 * tiles, 8, 128), jnp.float32)
    half = BLOCK // 2
    near = [(own, 0, 0, 0, 0), (column, 0, 0, 0, 1)]
    staged = rows == 4
    if staged:
        sums = gradient_sums(place, field, sums, near, shape, window, False)
    lower = jnp.concatenate([own_by_row[..., :half], by_row[..., :half]])
    upper = jnp.concatenate([own_by_par[..., half:], by_par[..., half:]])
    corner = lax.ppermute(lower, "par", swap), lax.ppermute(upper, "row", swap)
    beside = [
        [(own_by_row, 1, 0, 0, 0), (by_row, 1, 0, 0, 1)],
        [(own_by_par, 0, 1, 0, 0), (by_par, 0, 1, 0, 1)],
    ]
    if staged:
        for part in beside:
            sums = gradient_sums(place, field, sums, part, shape, window, False)
        corner, sums = lax.optimization_barrier((corner, sums))
    far = [(corner[0], 1, 1, 0, 0), (corner[1], 1, 1, half, 0)]
    part = far if staged else near + beside[0] + beside[1] + far
    sums = gradient_sums(place, field, sums, part, shape, window, True)

    sums = jnp.where(par == 0, sums, sums[::-1])
    sums = jnp.where(row == 0, sums, sums[:, ::-1])
    kept = jnp.where(par == 0, sums[:2], sums[2:])
    given = jnp.where(par == 0, sums[2:], sums[:2])
    total = kept + lax.ppermute(kept, "row", swap) + lax.ppermute(given, "par", swap)
    total = total + lax.ppermute(given, ("row", "par"), [(0, 3), (1, 2), (2, 1), (3, 0)])
    for turn in rotations(total, "mem"):
        total = total + turn
    return total * cell_weight


def solution(mesh):
    elec, space = mesh.devices.shape
    names = ("row", "mem", "pair", "par")
    finer = Mesh(mesh.devices.reshape(2, elec // 2, space // 2, 2), names)
    e, s = names[:2], names[2:]
    placed = (P(e, s, None, None), P(), P(), P(s, None, None))
    return jax.shard_map(local, mesh=finer, in_specs=placed, out_specs=P(s, None, None), check_vma=False)
```
